512 devices in a mesh: term: 8 (over y, core), sector: 64 (over x, z).
Axes of the slice: x: 4, y: 4, z: 16, core: 2. Of those that a mesh axis runs over, the one named last changes fastest.
Arguments:
- vectors: bfloat16 [3, 256, 256, 256], P(None, 'sector'), may hold values from -128 to 128
- dims: int32 [256, 2], P('sector'), may hold values from 64 to 256, as said below
- offsets: int32 [32], P('term'), may hold values from -2 to 2, as said below
- left_env: bfloat16 [32, 256, 256, 256], P('term', 'sector'), may hold values from -0.0625 to 0.0625
- right_env: bfloat16 [32, 256, 256, 256], P('term', 'sector'), may hold values from -0.375 to 0.375
Outputs:
- products: bfloat16 [3, 256, 256, 256], P(None, 'sector', 'term')
- subspace: float32 [3, 3], replicated
The draws below stay inside these ranges and needn't reach their ends.
Inputs may be any that keep to these rules, and one draw needn't show every extreme that they name: `dims`: each sector block has at most 256 rows and columns; some sector has exactly 256 of both. `offsets`: some term has offset -2 and some term +2.
All inputs are finite; a program needn't handle non-finite values.
Results may differ from the reference program's by a relative error of at most 0.011.
Values may be sent and summed in bfloat16 or wider, within the bound.
A program may use at most 64 MiB of HBM per device.

```python
import jax
import jax.numpy as jnp
from jax import lax

BLK = 256
REACH = 2
NVEC = 3
SECTORS = 256
TERMS = 32


def draw_dims(key, part):
    key = jax.random.fold_in(key, 11)
    first, second = jax.random.split(key)
    values = jax.random.randint(first, (SECTORS, 2), BLK // 4, BLK + 1)
    chosen = jax.random.randint(second, (), 0, SECTORS)
    return values.at[chosen].set(BLK).astype(jnp.int32)


def draw_offsets(key, part):
    key = jax.random.fold_in(key, 12)
    key = jax.random.fold_in(key, 7919)
    first, second, third = jax.random.split(key, 3)
    values = jax.random.randint(first, (TERMS,), 0 - REACH, REACH + 1)
    extra = jax.random.randint(third, (TERMS,), 0, 2 * REACH + 1)
    values = (values + extra + 2 * REACH) % (2 * REACH + 1) - REACH
    order = jax.random.permutation(second, TERMS)
    values = values.at[order[0]].set(0 - REACH).at[order[1]].set(REACH)
    return values.astype(jnp.int32)


def draw_vectors(key, part):
    key = jax.random.fold_in(key, 13)
    keys = jax.random.split(key, 3)
    shape = (NVEC, SECTORS, BLK, BLK)
    base = jax.random.truncated_normal(keys[0], -4.0, 4.0, shape, jnp.float32)
    spread = 1.15
    rising = 10.0 ** (jnp.arange(SECTORS, dtype=jnp.float32) / max(SECTORS - 1, 1) - 0.5)
    row_scale = jnp.exp(jax.random.uniform(keys[1], (NVEC, SECTORS, BLK, 1), jnp.float32, -spread, spread))
    col_scale = jnp.exp(jax.random.uniform(keys[2], (NVEC, SECTORS, 1, BLK), jnp.float32, -spread, spread))
    values = base * rising[None, :, None, None] * row_scale * col_scale
    return jnp.clip(values, -128.0, 128.0).astype(jnp.bfloat16)


def block_scale(own_key, shape, shards, low, high):
    level = 1.0
    for axis_at, shards_of in shards:
        heights = jax.random.uniform(jax.random.fold_in(jax.random.fold_in(own_key, 6), axis_at), (shards_of,), jnp.float32, low / len(shards), high / len(shards))
        level = level * jnp.repeat(jnp.exp(heights), shape[axis_at] // shards_of).reshape((-1,) + (1,) * (len(shape) - 1 - axis_at))
    return level


def scatter_about(rng, shape, scale, limit, pieces=(), held_as=jnp.bfloat16):
    factor_of = block_scale(rng, shape, pieces, -0.22, 0.18) if pieces else 1.0
    values = jax.random.normal(rng, shape, jnp.float32) * scale * factor_of
    return jnp.minimum(jnp.maximum(values, -limit), limit).astype(held_as)


def setup_inputs(seed: int = 0) -> dict:
    streams_of = jax.random.split(jax.random.key(seed), 6)
    vectors = draw_vectors(jax.random.fold_in(streams_of[5], 71), 0)
    dims = draw_dims(jax.random.fold_in(streams_of[5], 71), 0)
    offsets = draw_offsets(jax.random.fold_in(streams_of[5], 71), 0)
    left_env = scatter_about(streams_of[3], (TERMS, SECTORS, BLK, BLK), (BLK * TERMS) ** -0.5, 0.0625, ((0, 8), (1, 64)))
    right_env = scatter_about(streams_of[4], (TERMS, SECTORS, BLK, BLK), BLK ** -0.5, 0.375, ((0, 8), (1, 64)))
    return dict(vectors=vectors, dims=dims, offsets=offsets, left_env=left_env, right_env=right_env)


def block_mask(dims, size):
    rows = jnp.arange(size, dtype=jnp.int32)
    return (rows[None, :, None] < dims[:, 0][:, None, None]) & (rows[None, None, :] < dims[:, 1][:, None, None])


def reference(vectors, dims, offsets, left_env, right_env):
    mask = block_mask(dims, BLK)
    psi = jnp.where(mask[None], vectors, jnp.zeros_like(vectors))
    padded = jnp.pad(psi, ((0, 0), (REACH, REACH), (0, 0), (0, 0)))

    def step(total, items):
        shift_by, lenv, renv = items
        source = lax.dynamic_slice_in_dim(padded, (REACH - shift_by).astype(jnp.int32), SECTORS, 1)
        inner = jnp.einsum('vsab,scb->vsac', source.astype(jnp.float32), renv.astype(jnp.float32)).astype(jnp.bfloat16)
        return total + jnp.einsum('sda,vsac->vsdc', lenv.astype(jnp.float32), inner.astype(jnp.float32)), None

    start = jnp.zeros((NVEC, SECTORS, BLK, BLK), jnp.float32)
    total, unused = lax.scan(step, start, (offsets, left_env, right_env))
    products = jnp.where(mask[None], total, jnp.zeros_like(total)).astype(jnp.bfloat16)
    subspace = jnp.einsum('isab,jsab->ij', psi.astype(jnp.float32), total)
    return products, subspace
```

```python
import jax
import jax.numpy as jnp
from jax import lax
from jax.experimental import pallas as pl
from jax.experimental.pallas import tpu as pltpu
from jax.sharding import PartitionSpec as P

MESH = pl.DeviceIdType.MESH
NV = 3
F32 = jnp.float32
BF16 = jnp.bfloat16


def dot_nt(a, b):
    return lax.dot_general(a, b, (((1,), (1,)), ((), ())), preferred_element_type=F32)


def make_kernel(nz, nx):
    nsec = nz * nx

    def kernel(dims, offsets, vectors, lenv, renv, prod, sub,
               ext0, ext1, ext2, part0, part1, part2, lbuf, rbuf,
               sibrx, ysrc, yrx, ar1, ar2, ar3,
               vec_sem, env_sem, zs_sem, zr_sem, fs_sem, fr_sem, ss_sem, sr_sem, ys_sem, yr_sem,
               as_sem, a_sem, relay):
        ext = (ext0, ext1, ext2)
        part = (part0, part1, part2)
        k = lax.axis_index("term")
        g = lax.axis_index("sector")
        y = k // 2
        c = lax.rem(k, 2)
        sib = k + 1 - 2 * c
        zbase = (g // nz) * nz
        zi = lax.rem(g, nz)

        def zpeer(d):
            return zbase + lax.rem(zi + d + nz, nz)

        def ypeer(d):
            return lax.rem(k + 2 * d + 8, 8)

        def term_peer(d):
            return lax.rem(k + d, 8)

        def x_peer(d):
            return lax.rem(g + nz * d, nsec)

        nxt = lax.rem(g + 1, nsec)
        prv = lax.rem(g + nsec - 1, nsec)

        def dev(kk, gg):
            return {"term": kk, "sector": gg}

        def remote(src, dst, s_sem, r_sem, kk, gg):
            return pltpu.make_async_remote_copy(
                src_ref=src, dst_ref=dst, send_sem=s_sem, recv_sem=r_sem,
                device_id=dev(kk, gg), device_id_type=MESH)

        vec_cp = [pltpu.make_async_copy(vectors.at[v], ext[v].at[pl.ds(2, 4)], vec_sem.at[v])
                  for v in range(NV)]
        for cp in vec_cp:
            cp.start()
        renv_cp = pltpu.make_async_copy(renv, rbuf, env_sem.at[0])
        lenv_cp = pltpu.make_async_copy(lenv, lbuf, env_sem.at[1])
        renv_cp.start()
        lenv_cp.start()

        barrier = pltpu.get_barrier_semaphore()
        near = ([(term_peer(d), g) for d in range(1, 8)] + [(k, nxt), (k, prv), (k, zpeer(1)), (k, zpeer(-1))]
                + [(k, x_peer(d)) for d in range(1, nx)])
        for p in near:
            pl.semaphore_signal(barrier, inc=1, device_id=dev(*p), device_id_type=MESH)

        masks = []
        row_id = lax.broadcasted_iota(jnp.int32, (256, 256), 0)
        col_id = lax.broadcasted_iota(jnp.int32, (256, 256), 1)
        for s in range(4):
            inside = (row_id < dims[0, s]) & (col_id < dims[1, s])
            masks.append(jnp.where(inside, 1.0, 0.0).astype(BF16))
        for v in range(NV):
            vec_cp[v].wait()
            for s in range(4):
                ext[v][2 + s] = ext[v][2 + s] * masks[s]
        pl.semaphore_wait(barrier, len(near))

        up, down = [], []
        for v in range(NV):
            a = remote(ext[v].at[4 + c], ext[v].at[c], zs_sem.at[v, 0], zr_sem.at[v, 0], k, nxt)
            b = remote(ext[v].at[2 + c], ext[v].at[6 + c], zs_sem.at[v, 1], zr_sem.at[v, 1], k, prv)
            a.start()
            b.start()
            up.append(a)
            down.append(b)

        def tell(step, dist):
            for d in (dist, -dist):
                pl.semaphore_signal(relay.at[step], inc=1, device_id=dev(k, zpeer(d)), device_id_type=MESH)

        def hear(step):
            pl.semaphore_wait(relay.at[step], 2)

        tell(0, 1)

        sib_cp, y_cp = [], []

        def sib_send(v):
            cp = remote(part[v].at[:, :, 1 - c], sibrx.at[v], ss_sem.at[v], sr_sem.at[v], sib, g)
            cp.start()
            sib_cp.append(cp)

        def chip_sum(v):
            sib_cp[v].wait()
            for yy in range(4):
                for s in range(4):
                    both = part[v][s, yy, c].astype(F32) + sibrx[v, s, yy].astype(F32)
                    ysrc[v, yy, s] = both.astype(BF16)
            for d in (2, 1, 3):
                dest = lax.rem(y + d, 4)
                cp = remote(ysrc.at[v, dest], yrx.at[v, d - 1], ys_sem.at[v, d - 1], yr_sem.at[v, d - 1],
                            ypeer(d), g)
                cp.start()
                y_cp.append(cp)

        accs = {}
        for v in range(NV):
            if v >= 1:
                chip_sum(v - 1)
            up[v].wait_recv()
            down[v].wait_recv()
            fa = remote(ext[v].at[c], ext[v].at[c], fs_sem.at[v, 0], fr_sem.at[v, 0], sib, g)
            fb = remote(ext[v].at[6 + c], ext[v].at[6 + c], fs_sem.at[v, 1], fr_sem.at[v, 1], sib, g)
            fa.start()
            fb.start()
            fa.wait()
            fb.wait()

            @pl.when(g == 0)
            def _():
                ext[v][0:2] = jnp.zeros((2, 256, 256), BF16)

            @pl.when(g == nsec - 1)
            def _():
                ext[v][6:8] = jnp.zeros((2, 256, 256), BF16)

            if v == 0:
                renv_cp.wait()
                lenv_cp.wait()
            for s in range(4):
                tot = None
                for t in range(4):
                    inner = dot_nt(ext[v][2 + s - offsets[t]], rbuf[t, s]).astype(BF16)
                    term = jnp.dot(lbuf[t, s], inner, preferred_element_type=F32)
                    tot = term if tot is None else tot + term
                part[v][s] = tot.reshape(4, 2, 32, 256).astype(BF16)
                for i in range(NV):
                    z = ext[i][2 + s].astype(F32) * tot
                    z = jnp.sum(z.reshape(32, 8, 256), axis=0)
                    z = z[:, :128] + z[:, 128:]
                    accs[i, v] = z if s == 0 else accs[i, v] + z
            sib_send(v)
            if v < 2:
                hear(v)
                tell(v + 1, 2 * (v + 1))

        rows = jnp.concatenate(
            [jnp.sum(accs[i, j], axis=0, keepdims=True) for i in range(NV) for j in range(NV)], axis=0)
        sums = jnp.sum(rows, axis=1, keepdims=True)
        diag = (lax.broadcasted_iota(jnp.int32, (9, 128), 0)
                == lax.broadcasted_iota(jnp.int32, (9, 128), 1))
        ar1[0] = jnp.sum(jnp.where(diag, sums, 0.0), axis=0, keepdims=True)

        def spread(buf, n, sem, peer):
            cps = [remote(buf.at[0], buf.at[d], as_sem.at[sem], a_sem.at[sem], *peer(d)) for d in range(1, n)]
            for cp in cps:
                cp.start()

        def gather(buf, n, sem):
            pltpu.make_async_copy(buf.at[pl.ds(1, n - 1)], buf.at[pl.ds(1, n - 1)], a_sem.at[sem]).wait()
            return jnp.sum(buf[...], axis=0)

        def drain(buf, n, sem):
            pltpu.make_async_copy(buf.at[pl.ds(1, n - 1)], buf.at[pl.ds(1, n - 1)], as_sem.at[sem]).wait()

        spread(ar1, 8, 0, lambda d: (term_peer(d), g))
        chip_sum(2)
        ar2[0] = gather(ar1, 8, 0)
        spread(ar2, nx, 1, lambda d: (k, x_peer(d)))
        ar3[0] = gather(ar2, nx, 1)
        hear(2)
        spread(ar3, nz, 2, lambda d: (k, zpeer(d)))

        lane = lax.broadcasted_iota(jnp.int32, (32, 256), 1)
        rown = lax.broadcasted_iota(jnp.int32, (32, 256), 0) + k * 32
        for v in range(NV):
            for j in range(3):
                y_cp[3 * v + j].wait()
            for s in range(4):
                tot = ysrc[v, y, s].astype(F32)
                for d in range(3):
                    tot = tot + yrx[v, d, s].astype(F32)
                inside = (rown < dims[0, s]) & (lane < dims[1, s])
                prod[v, s] = jnp.where(inside, tot, 0.0).astype(BF16)
        for v in range(NV):
            up[v].wait_send()
            down[v].wait_send()
        drain(ar1, 8, 0)
        drain(ar2, nx, 1)
        drain(ar3, nz, 2)
        sub[...] = gather(ar3, nz, 2)

    return kernel


def solution(mesh):
    nz = 16
    nx = mesh.shape["sector"] // nz
    vmem = pl.BlockSpec(memory_space=pltpu.VMEM)
    smem = pl.BlockSpec(memory_space=pltpu.SMEM)
    hbm = pl.BlockSpec(memory_space=pl.ANY)
    dma = pltpu.SemaphoreType.DMA

    def body(vectors, dims, offsets, left_env, right_env):
        prod, row = pl.pallas_call(
            make_kernel(nz, nx),
            out_shape=(jax.ShapeDtypeStruct((NV, 4, 32, 256), BF16),
                       jax.ShapeDtypeStruct((1, 128), F32)),
            in_specs=[smem, smem, hbm, hbm, hbm],
            out_specs=(vmem, vmem),
            scratch_shapes=(
                [pltpu.VMEM((8, 256, 256), BF16)] * 3
                + [pltpu.VMEM((4, 4, 2, 32, 256), BF16)] * 3
                + [pltpu.VMEM((4, 4, 256, 256), BF16)] * 2
                + [pltpu.VMEM((NV, 4, 4, 32, 256), BF16),
                   pltpu.VMEM((NV, 4, 4, 32, 256), BF16),
                   pltpu.VMEM((NV, 3, 4, 32, 256), BF16),
                   pltpu.VMEM((8, 1, 128), F32),
                   pltpu.VMEM((nx, 1, 128), F32),
                   pltpu.VMEM((nz, 1, 128), F32),
                   dma((NV,)), dma((2,)), dma((NV, 2)), dma((NV, 2)), dma((NV, 2)), dma((NV, 2)),
                   dma((NV,)), dma((NV,)), dma((NV, 3)), dma((NV, 3)),
                   dma((3,)), dma((3,)), pltpu.SemaphoreType.REGULAR((3,))]),
            compiler_params=pltpu.CompilerParams(
                collective_id=0, has_side_effects=True, vmem_limit_bytes=56 << 20),
        )(dims.T, offsets, vectors, left_env, right_env)
        return prod, row[0, :9].reshape(3, 3)

    return jax.shard_map(
        body,
        mesh=mesh,
        in_specs=(
            P(None, "sector", None, None),
            P("sector", None),
            P("term"),
            P("term", "sector", None, None),
            P("term", "sector", None, None),
        ),
        out_specs=(P(None, "sector", "term", None), P()),
        check_vma=False,
    )
```

```python
import jax
import jax.numpy as jnp
from jax import lax
from jax.experimental import pallas as pl
from jax.experimental.pallas import tpu as pltpu
from jax.sharding import PartitionSpec as P

MESH = pl.DeviceIdType.MESH
NV = 3
F32 = jnp.float32
BF16 = jnp.bfloat16


def dot_nt(a, b):
    return lax.dot_general(a, b, (((1,), (1,)), ((), ())), preferred_element_type=F32)


def make_kernel(nz, nx):
    nsec = nz * nx

    def kernel(dims_hbm, offsets_hbm, vectors, lenv, renv, prod, sub,
               ext0, ext1, ext2, part0, part1, part2, lbuf, rbuf,
               sibrx, ysrc, yrx, ar1, ar3, dims, offsets,
               vec_sem, env_sem, int_sem, zs_sem, zr_sem, fs_sem, fr_sem, ss_sem, sr_sem, ys_sem, yr_sem,
               as_sem, a_sem, relay):
        ext = (ext0, ext1, ext2)
        part = (part0, part1, part2)
        k = lax.axis_index("term")
        g = lax.axis_index("sector")
        y = k // 2
        c = lax.rem(k, 2)
        sib = k + 1 - 2 * c
        zbase = (g // nz) * nz
        zi = lax.rem(g, nz)

        def zpeer(d):
            return zbase + lax.rem(zi + d + nz, nz)

        def ypeer(d):
            return lax.rem(k + 2 * d + 8, 8)

        def term_peer(d):
            return lax.rem(k + d, 8)

        def x_peer(d):
            return lax.rem(g + nz * d, nsec)

        nxt = lax.rem(g + 1, nsec)
        prv = lax.rem(g + nsec - 1, nsec)

        def dev(kk, gg):
            return {"term": kk, "sector": gg}

        def remote(src, dst, s_sem, r_sem, kk, gg):
            return pltpu.make_async_remote_copy(
                src_ref=src, dst_ref=dst, send_sem=s_sem, recv_sem=r_sem,
                device_id=dev(kk, gg), device_id_type=MESH)

        barrier = pltpu.get_barrier_semaphore()
        beside = [(sib, g), (ypeer(1), g), (ypeer(-1), g), (k, x_peer(1)), (k, x_peer(nx - 1)),
                  (k, zpeer(1)), (k, zpeer(-1))]
        near = beside + [(k, nxt), (k, prv)]
        for p in near:
            pl.semaphore_signal(barrier, inc=1, device_id=dev(*p), device_id_type=MESH)

        dims_cp = pltpu.make_async_copy(dims_hbm, dims, int_sem.at[0])
        offs_cp = pltpu.make_async_copy(offsets_hbm, offsets, int_sem.at[1])
        dims_cp.start()
        offs_cp.start()
        vec_cp = [pltpu.make_async_copy(vectors.at[v], ext[v].at[pl.ds(2, 4)], vec_sem.at[v])
                  for v in range(NV)]
        for cp in vec_cp:
            cp.start()
        renv_cp = pltpu.make_async_copy(renv, rbuf, env_sem.at[0])
        lenv_cp = pltpu.make_async_copy(lenv, lbuf, env_sem.at[1])
        renv_cp.start()
        lenv_cp.start()

        dims_cp.wait()
        offs_cp.wait()
        masks = []
        row_id = lax.broadcasted_iota(jnp.int32, (256, 256), 0)
        col_id = lax.broadcasted_iota(jnp.int32, (256, 256), 1)
        for s in range(4):
            inside = (row_id < dims[0, s]) & (col_id < dims[1, s])
            masks.append(jnp.where(inside, 1.0, 0.0).astype(BF16))
        for v in range(NV):
            vec_cp[v].wait()
            for s in range(4):
                ext[v][2 + s] = ext[v][2 + s] * masks[s]
        pl.semaphore_wait(barrier, len(near))

        up, down = [], []
        for v in range(NV):
            a = remote(ext[v].at[4 + c], ext[v].at[c], zs_sem.at[v, 0], zr_sem.at[v, 0], k, nxt)
            b = remote(ext[v].at[2 + c], ext[v].at[6 + c], zs_sem.at[v, 1], zr_sem.at[v, 1], k, prv)
            a.start()
            b.start()
            up.append(a)
            down.append(b)

        chain = [beside,
                 [(sib, g), (ypeer(2), g), (k, x_peer(2)), (k, zpeer(2)), (k, zpeer(-2))],
                 [(ypeer(2), g), (k, zpeer(4)), (k, zpeer(-4))]]

        def tell(step):
            for p in chain[step]:
                pl.semaphore_signal(relay.at[step], inc=1, device_id=dev(*p), device_id_type=MESH)

        def hear(step):
            pl.semaphore_wait(relay.at[step], len(chain[step]))

        tell(0)

        sib_cp, y_cp = [], []

        def sib_send(v):
            cp = remote(part[v].at[:, :, 1 - c], sibrx.at[v], ss_sem.at[v], sr_sem.at[v], sib, g)
            cp.start()
            sib_cp.append(cp)

        def chip_sum(v):
            sib_cp[v].wait()
            for yy in range(4):
                for s in range(4):
                    both = part[v][s, yy, c].astype(F32) + sibrx[v, s, yy].astype(F32)
                    ysrc[v, yy, s] = both.astype(BF16)
            for d in (2, 1, 3):
                dest = lax.rem(y + d, 4)
                cp = remote(ysrc.at[v, dest], yrx.at[v, d - 1], ys_sem.at[v, d - 1], yr_sem.at[v, d - 1],
                            ypeer(d), g)
                cp.start()
                y_cp.append(cp)

        accs = {}
        for v in range(NV):
            if v >= 1:
                chip_sum(v - 1)
            if v == 0:
                hear(0)
                tell(1)
            up[v].wait_recv()
            down[v].wait_recv()
            fa = remote(ext[v].at[c], ext[v].at[c], fs_sem.at[v, 0], fr_sem.at[v, 0], sib, g)
            fb = remote(ext[v].at[6 + c], ext[v].at[6 + c], fs_sem.at[v, 1], fr_sem.at[v, 1], sib, g)
            fa.start()
            fb.start()
            fa.wait()
            fb.wait()

            @pl.when(g == 0)
            def _():
                ext[v][0:2] = jnp.zeros((2, 256, 256), BF16)

            @pl.when(g == nsec - 1)
            def _():
                ext[v][6:8] = jnp.zeros((2, 256, 256), BF16)

            if v == 0:
                renv_cp.wait()
                lenv_cp.wait()
            for s in range(4):
                tot = None
                for t in range(4):
                    inner = dot_nt(ext[v][2 + s - offsets[t]], rbuf[t, s]).astype(BF16)
                    term = jnp.dot(lbuf[t, s], inner, preferred_element_type=F32)
                    tot = term if tot is None else tot + term
                part[v][s] = tot.reshape(4, 2, 32, 256).astype(BF16)
                for i in range(NV):
                    z = ext[i][2 + s].astype(F32) * tot
                    z = jnp.sum(z.reshape(32, 8, 256), axis=0)
                    z = z[:, :128] + z[:, 128:]
                    accs[i, v] = z if s == 0 else accs[i, v] + z
            sib_send(v)
            if v == 0:
                hear(1)
                tell(2)

        rows = jnp.concatenate(
            [jnp.sum(accs[i, j], axis=0, keepdims=True) for i in range(NV) for j in range(NV)], axis=0)
        sums = jnp.sum(rows, axis=1, keepdims=True)
        diag = (lax.broadcasted_iota(jnp.int32, (9, 128), 0)
                == lax.broadcasted_iota(jnp.int32, (9, 128), 1))
        ar1[0] = jnp.sum(jnp.where(diag, sums, 0.0), axis=0, keepdims=True)

        def spread(buf, sem, peers):
            for d, peer in peers:
                remote(buf.at[0], buf.at[d], as_sem.at[sem], a_sem.at[sem], *peer).start()

        def others(buf, sem):
            n = buf.shape[0] - 1
            return pltpu.make_async_copy(buf.at[pl.ds(1, n)], buf.at[pl.ds(1, n)], sem)

        hear(2)
        plane = sorted(((dx, dk) for dx in range(nx) for dk in range(8) if dx + dk),
                       key=lambda p: -(min(p[0], nx - p[0]) + min(p[1] // 2, 4 - p[1] // 2)))
        spread(ar1, 0, [(8 * dx + dk, (term_peer(dk), x_peer(dx))) for dx, dk in plane])
        chip_sum(2)
        others(ar1, a_sem.at[0]).wait()
        ar3[0] = jnp.sum(ar1[...], axis=0)
        line = sorted(range(1, nz), key=lambda d: -min(d, nz - d))
        spread(ar3, 1, [(d, (k, zpeer(d))) for d in line])

        lane = lax.broadcasted_iota(jnp.int32, (32, 256), 1)
        rown = lax.broadcasted_iota(jnp.int32, (32, 256), 0) + k * 32
        for v in range(NV):
            for j in range(3):
                y_cp[3 * v + j].wait()
            for s in range(4):
                tot = ysrc[v, y, s].astype(F32)
                for d in range(3):
                    tot = tot + yrx[v, d, s].astype(F32)
                inside = (rown < dims[0, s]) & (lane < dims[1, s])
                prod[v, s] = jnp.where(inside, tot, 0.0).astype(BF16)
        for v in range(NV):
            up[v].wait_send()
            down[v].wait_send()
        others(ar1, as_sem.at[0]).wait()
        others(ar3, as_sem.at[1]).wait()
        others(ar3, a_sem.at[1]).wait()
        sums = jnp.broadcast_to(jnp.sum(ar3[...], axis=0), (3, 128))
        r3 = lax.broadcasted_iota(jnp.int32, (3, 128), 0)
        l3 = lax.broadcasted_iota(jnp.int32, (3, 128), 1)
        full = jnp.zeros((3, 128), F32)
        for j in range(NV):
            col = jnp.sum(jnp.where(l3 == 3 * r3 + j, sums, 0.0), axis=1, keepdims=True)
            full = jnp.where(l3 == j, col, full)
        sub[...] = full[:, :3]

    return kernel


def hand_over(prod_in, sub_in, prod, sub):
    prod[...] = prod_in[...]
    sub[...] = sub_in[...]


def solution(mesh):
    nz = 16
    nx = mesh.shape["sector"] // nz
    vmem = pl.BlockSpec(memory_space=pltpu.VMEM)
    hbm = pl.BlockSpec(memory_space=pl.ANY)
    dma = pltpu.SemaphoreType.DMA

    def body(vectors, dims, offsets, left_env, right_env):
        prod, sub = pl.pallas_call(
            make_kernel(nz, nx),
            out_shape=(pltpu.VMEM((NV, 4, 32, 256), BF16), pltpu.VMEM((3, 3), F32)),
            in_specs=[hbm] * 5,
            out_specs=(vmem, vmem),
            scratch_shapes=(
                [pltpu.VMEM((8, 256, 256), BF16)] * 3
                + [pltpu.VMEM((4, 4, 2, 32, 256), BF16)] * 3
                + [pltpu.VMEM((4, 4, 256, 256), BF16)] * 2
                + [pltpu.VMEM((NV, 4, 4, 32, 256), BF16),
                   pltpu.VMEM((NV, 4, 4, 32, 256), BF16),
                   pltpu.VMEM((NV, 3, 4, 32, 256), BF16),
                   pltpu.VMEM((8 * nx, 1, 128), F32),
                   pltpu.VMEM((nz, 1, 128), F32),
                   pltpu.SMEM((2, 4), jnp.int32), pltpu.SMEM((4,), jnp.int32),
                   dma((NV,)), dma((2,)), dma((2,)),
                   dma((NV, 2)), dma((NV, 2)), dma((NV, 2)), dma((NV, 2)),
                   dma((NV,)), dma((NV,)), dma((NV, 3)), dma((NV, 3)),
                   dma((2,)), dma((2,)), pltpu.SemaphoreType.REGULAR((3,))]),
            compiler_params=pltpu.CompilerParams(
                collective_id=0, has_side_effects=True, vmem_limit_bytes=56 << 20),
        )(dims.T, offsets, vectors, left_env, right_env)
        return pl.pallas_call(
            hand_over,
            out_shape=(jax.ShapeDtypeStruct((NV, 4, 32, 256), BF16), jax.ShapeDtypeStruct((3, 3), F32)),
            in_specs=[vmem, vmem],
            out_specs=(vmem, vmem),
            compiler_params=pltpu.CompilerParams(vmem_limit_bytes=2 << 20),
        )(prod, sub)

    return jax.shard_map(
        body,
        mesh=mesh,
        in_specs=(
            P(None, "sector", None, None),
            P("sector", None),
            P("term"),
            P("term", "sector", None, None),
            P("term", "sector", None, None),
        ),
        out_specs=(P(None, "sector", "term", None), P()),
        check_vma=False,
    )
```

```python
import jax
import jax.numpy as jnp
from jax import lax
from jax.experimental import pallas as pl
from jax.experimental.pallas import tpu as pltpu
from jax.sharding import PartitionSpec as P

MESH = pl.DeviceIdType.MESH
NV = 3
F32 = jnp.float32
BF16 = jnp.bfloat16


def dot_nt(a, b):
    return lax.dot_general(a, b, (((1,), (1,)), ((), ())), preferred_element_type=F32)


def make_kernel(nz, nx):
    nsec = nz * nx

    def kernel(dims_hbm, offsets_hbm, vectors, lenv, renv, prod, sub,
               ext0, ext1, ext2, part0, part1, part2, lbuf, rbuf,
               sibrx, ysrc, yrx, ar1, ar3, dims, offsets,
               vec_sem, env_sem, int_sem, zs_sem, zr_sem, hs_sem, hr_sem, fs_sem, fr_sem, ss_sem, sr_sem, ys_sem, yr_sem,
               as_sem, a_sem, relay):
        ext = (ext0, ext1, ext2)
        part = (part0, part1, part2)
        k = lax.axis_index("term")
        g = lax.axis_index("sector")
        y = k // 2
        c = lax.rem(k, 2)
        sib = k + 1 - 2 * c
        zbase = (g // nz) * nz
        zi = lax.rem(g, nz)

        def zpeer(d):
            return zbase + lax.rem(zi + d + nz, nz)

        def ypeer(d):
            return lax.rem(k + 2 * d + 8, 8)

        def term_peer(d):
            return lax.rem(k + d, 8)

        def x_peer(d):
            return lax.rem(g + nz * d, nsec)

        nxt = lax.rem(g + 1, nsec)
        prv = lax.rem(g + nsec - 1, nsec)

        def dev(kk, gg):
            return {"term": kk, "sector": gg}

        def remote(src, dst, s_sem, r_sem, kk, gg):
            return pltpu.make_async_remote_copy(
                src_ref=src, dst_ref=dst, send_sem=s_sem, recv_sem=r_sem,
                device_id=dev(kk, gg), device_id_type=MESH)

        barrier = pltpu.get_barrier_semaphore()
        beside = [(sib, g), (ypeer(1), g), (ypeer(-1), g), (k, x_peer(1)), (k, x_peer(nx - 1)),
                  (k, zpeer(1)), (k, zpeer(-1))]
        near = beside + [(k, nxt), (k, prv)]
        for p in near:
            pl.semaphore_signal(barrier, inc=1, device_id=dev(*p), device_id_type=MESH)

        dims_cp = pltpu.make_async_copy(dims_hbm, dims, int_sem.at[0])
        offs_cp = pltpu.make_async_copy(offsets_hbm, offsets, int_sem.at[1])
        dims_cp.start()
        offs_cp.start()
        vec_cp = [pltpu.make_async_copy(vectors.at[v], ext[v].at[pl.ds(2, 4)], vec_sem.at[v])
                  for v in range(NV)]
        for v in (1, 0, 2):
            vec_cp[v].start()
        renv_cp = pltpu.make_async_copy(renv, rbuf, env_sem.at[0])
        lenv_cp = pltpu.make_async_copy(lenv, lbuf, env_sem.at[1])

        dims_cp.wait()
        offs_cp.wait()
        masks = []
        row_id = lax.broadcasted_iota(jnp.int32, (256, 256), 0)
        col_id = lax.broadcasted_iota(jnp.int32, (256, 256), 1)
        for s in range(4):
            inside = (row_id < dims[0, s]) & (col_id < dims[1, s])
            masks.append(jnp.where(inside, 1.0, 0.0).astype(BF16))
        def masked(v):
            vec_cp[v].wait()
            for s in range(4):
                ext[v][2 + s] = ext[v][2 + s] * masks[s]

        masked(1)
        pl.semaphore_wait(barrier, len(near))

        def quarter(v, sector, yy):
            return ext[v].at[sector, pl.ds(pl.multiple_of(64 * yy, 64), 64)]

        def ahead(n, src, dst):
            cps = [remote(src(4 + c), dst(c), zs_sem.at[n, 0], zr_sem.at[n, 0], k, nxt),
                   remote(src(2 + c), dst(6 + c), zs_sem.at[n, 1], zr_sem.at[n, 1], k, prv)]
            for cp in cps:
                cp.start()
            return cps

        opp = lax.rem(y + 2, 4)
        z_own = ahead(3, lambda e: quarter(1, e, y), lambda e: quarter(1, e, y))
        masked(0)
        z_cp = {0: ahead(0, lambda e: ext[0].at[e], lambda e: ext[0].at[e])}
        z_cp[1] = ahead(1, lambda e: quarter(1, e, opp), lambda e: quarter(1, e, opp))
        masked(2)
        z_cp[2] = ahead(2, lambda e: ext[2].at[e], lambda e: ext[2].at[e])

        renv_cp.start()
        lenv_cp.start()

        chain = [beside,
                 [(sib, g), (ypeer(2), g), (k, x_peer(2)), (k, zpeer(2)), (k, zpeer(-2))],
                 [(ypeer(2), g), (k, zpeer(4)), (k, zpeer(-4))]]

        def tell(step):
            for p in chain[step]:
                pl.semaphore_signal(relay.at[step], inc=1, device_id=dev(*p), device_id_type=MESH)

        def hear(step):
            pl.semaphore_wait(relay.at[step], len(chain[step]))

        tell(0)

        sib_cp, y_cp = [], []

        def sib_send(v):
            cp = remote(part[v].at[:, :, 1 - c], sibrx.at[v], ss_sem.at[v], sr_sem.at[v], sib, g)
            cp.start()
            sib_cp.append(cp)

        def chip_sum(v):
            sib_cp[v].wait()
            for yy in range(4):
                for s in range(4):
                    both = part[v][s, yy, c].astype(F32) + sibrx[v, s, yy].astype(F32)
                    ysrc[v, yy, s] = both.astype(BF16)
            for d in (2, 1, 3):
                dest = lax.rem(y + d, 4)
                cp = remote(ysrc.at[v, dest], yrx.at[v, d - 1], ys_sem.at[v, d - 1], yr_sem.at[v, d - 1],
                            ypeer(d), g)
                cp.start()
                y_cp.append(cp)

        hear(0)
        tell(1)
        for cp in z_own:
            cp.wait_recv()
        h_cp = []
        for side, sector in enumerate((c, 6 + c)):
            for way, d in enumerate((1, -1)):
                cp = remote(quarter(1, sector, y), quarter(1, sector, y), hs_sem.at[side, way],
                            hr_sem.at[side, way], ypeer(d), g)
                cp.start()
                h_cp.append(cp)

        accs = {}
        passing = {}

        def pass_on(v):
            for cp in z_cp[v] + (h_cp if v == 1 else []):
                cp.wait_recv()
            passing[v] = [remote(ext[v].at[c], ext[v].at[c], fs_sem.at[v, 0], fr_sem.at[v, 0], sib, g),
                          remote(ext[v].at[6 + c], ext[v].at[6 + c], fs_sem.at[v, 1], fr_sem.at[v, 1], sib, g)]
            for cp in passing[v]:
                cp.start()

        def complete(v):
            for cp in passing[v]:
                cp.wait()
            if v == 1:
                for cp in h_cp:
                    cp.wait_send()

            @pl.when(g == 0)
            def _():
                ext[v][0:2] = jnp.zeros((2, 256, 256), BF16)

            @pl.when(g == nsec - 1)
            def _():
                ext[v][6:8] = jnp.zeros((2, 256, 256), BF16)

        def products(v, sectors):
            for s in sectors:
                tot = None
                for t in range(4):
                    inner = dot_nt(ext[v][2 + s - offsets[t]], rbuf[t, s]).astype(BF16)
                    term = jnp.dot(lbuf[t, s], inner, preferred_element_type=F32)
                    tot = term if tot is None else tot + term
                part[v][s] = tot.reshape(4, 2, 32, 256).astype(BF16)
                for i in range(NV):
                    z = ext[i][2 + s].astype(F32) * tot
                    z = jnp.sum(z.reshape(32, 8, 256), axis=0)
                    z = z[:, :128] + z[:, 128:]
                    accs[i, v] = z if s == 0 else accs[i, v] + z

        pass_on(0)
        renv_cp.wait()
        lenv_cp.wait()
        complete(0)
        products(0, (0, 1))
        pass_on(1)
        products(0, (2, 3))
        sib_send(0)
        hear(1)
        tell(2)
        complete(1)
        products(1, (0, 1))
        pass_on(2)
        products(1, (2, 3))
        sib_send(1)
        chip_sum(0)
        complete(2)
        products(2, (0, 1, 2, 3))
        sib_send(2)

        rows = jnp.concatenate(
            [jnp.sum(accs[i, j], axis=0, keepdims=True) for i in range(NV) for j in range(NV)], axis=0)
        sums = jnp.sum(rows, axis=1, keepdims=True)
        diag = (lax.broadcasted_iota(jnp.int32, (9, 128), 0)
                == lax.broadcasted_iota(jnp.int32, (9, 128), 1))
        ar1[0] = jnp.sum(jnp.where(diag, sums, 0.0), axis=0, keepdims=True)

        def spread(buf, sem, peers):
            for d, peer in peers:
                remote(buf.at[0], buf.at[d], as_sem.at[sem], a_sem.at[sem], *peer).start()

        def others(buf, sem):
            n = buf.shape[0] - 1
            return pltpu.make_async_copy(buf.at[pl.ds(1, n)], buf.at[pl.ds(1, n)], sem)

        hear(2)
        plane = sorted(((dx, dk) for dx in range(nx) for dk in range(8) if dx + dk),
                       key=lambda p: -(min(p[0], nx - p[0]) + min(p[1] // 2, 4 - p[1] // 2)))
        spread(ar1, 0, [(8 * dx + dk, (term_peer(dk), x_peer(dx))) for dx, dk in plane])
        chip_sum(1)
        chip_sum(2)
        others(ar1, a_sem.at[0]).wait()
        ar3[0] = jnp.sum(ar1[...], axis=0)
        line = sorted(range(1, nz), key=lambda d: -min(d, nz - d))
        spread(ar3, 1, [(d, (k, zpeer(d))) for d in line])

        lane = lax.broadcasted_iota(jnp.int32, (32, 256), 1)
        rown = lax.broadcasted_iota(jnp.int32, (32, 256), 0) + k * 32
        for v in range(NV):
            for j in range(3):
                y_cp[3 * v + j].wait()
            for s in range(4):
                tot = ysrc[v, y, s].astype(F32)
                for d in range(3):
                    tot = tot + yrx[v, d, s].astype(F32)
                inside = (rown < dims[0, s]) & (lane < dims[1, s])
                prod[v, s] = jnp.where(inside, tot, 0.0).astype(BF16)
        for cp in z_own + z_cp[0] + z_cp[1] + z_cp[2]:
            cp.wait_send()
        others(ar1, as_sem.at[0]).wait()
        others(ar3, as_sem.at[1]).wait()
        others(ar3, a_sem.at[1]).wait()
        sums = jnp.broadcast_to(jnp.sum(ar3[...], axis=0), (3, 128))
        r3 = lax.broadcasted_iota(jnp.int32, (3, 128), 0)
        l3 = lax.broadcasted_iota(jnp.int32, (3, 128), 1)
        full = jnp.zeros((3, 128), F32)
        for j in range(NV):
            col = jnp.sum(jnp.where(l3 == 3 * r3 + j, sums, 0.0), axis=1, keepdims=True)
            full = jnp.where(l3 == j, col, full)
        sub[...] = full[:, :3]

    return kernel


def hand_over(prod_in, sub_in, prod, sub):
    prod[...] = prod_in[...]
    sub[...] = sub_in[...]


def solution(mesh):
    nz = 16
    nx = mesh.shape["sector"] // nz
    vmem = pl.BlockSpec(memory_space=pltpu.VMEM)
    hbm = pl.BlockSpec(memory_space=pl.ANY)
    dma = pltpu.SemaphoreType.DMA

    def body(vectors, dims, offsets, left_env, right_env):
        prod, sub = pl.pallas_call(
            make_kernel(nz, nx),
            out_shape=(pltpu.VMEM((NV, 4, 32, 256), BF16), pltpu.VMEM((3, 3), F32)),
            in_specs=[hbm] * 5,
            out_specs=(vmem, vmem),
            scratch_shapes=(
                [pltpu.VMEM((8, 256, 256), BF16)] * 3
                + [pltpu.VMEM((4, 4, 2, 32, 256), BF16)] * 3
                + [pltpu.VMEM((4, 4, 256, 256), BF16)] * 2
                + [pltpu.VMEM((NV, 4, 4, 32, 256), BF16),
                   pltpu.VMEM((NV, 4, 4, 32, 256), BF16),
                   pltpu.VMEM((NV, 3, 4, 32, 256), BF16),
                   pltpu.VMEM((8 * nx, 1, 128), F32),
                   pltpu.VMEM((nz, 1, 128), F32),
                   pltpu.SMEM((2, 4), jnp.int32), pltpu.SMEM((4,), jnp.int32),
                   dma((NV,)), dma((2,)), dma((2,)),
                   dma((4, 2)), dma((4, 2)), dma((2, 2)), dma((2, 2)), dma((NV, 2)), dma((NV, 2)),
                   dma((NV,)), dma((NV,)), dma((NV, 3)), dma((NV, 3)),
                   dma((2,)), dma((2,)), pltpu.SemaphoreType.REGULAR((3,))]),
            compiler_params=pltpu.CompilerParams(
                collective_id=0, has_side_effects=True, vmem_limit_bytes=56 << 20),
        )(dims.T, offsets, vectors, left_env, right_env)
        return pl.pallas_call(
            hand_over,
            out_shape=(jax.ShapeDtypeStruct((NV, 4, 32, 256), BF16), jax.ShapeDtypeStruct((3, 3), F32)),
            in_specs=[vmem, vmem],
            out_specs=(vmem, vmem),
            compiler_params=pltpu.CompilerParams(vmem_limit_bytes=2 << 20),
        )(prod, sub)

    return jax.shard_map(
        body,
        mesh=mesh,
        in_specs=(
            P(None, "sector", None, None),
            P("sector", None),
            P("term"),
            P("term", "sector", None, None),
            P("term", "sector", None, None),
        ),
        out_specs=(P(None, "sector", "term", None), P()),
        check_vma=False,
    )
```

```python
import jax
import jax.numpy as jnp
from jax import lax
from jax.experimental import pallas as pl
from jax.experimental.pallas import tpu as pltpu
from jax.sharding import PartitionSpec as P

MESH = pl.DeviceIdType.MESH
NV = 3
F32 = jnp.float32
BF16 = jnp.bfloat16


def dot_nt(a, b):
    return lax.dot_general(a, b, (((1,), (1,)), ((), ())), preferred_element_type=F32)


def make_kernel(nz, nx):
    nsec = nz * nx

    def kernel(dims_hbm, offsets_hbm, vectors, lenv, renv, prod, sub,
               ext0, ext1, ext2, part0, part1, part2, lbuf, rbuf,
               sibrx, ysrc, yrx, ar1, ar3, dims, offsets,
               vec_sem, env_sem, int_sem, zs_sem, zr_sem, hs_sem, hr_sem, fs_sem, fr_sem, ss_sem, sr_sem, ys_sem, yr_sem,
               as_sem, a_sem, relay):
        ext = (ext0, ext1, ext2)
        part = (part0, part1, part2)
        k = lax.axis_index("term")
        g = lax.axis_index("sector")
        y = k // 2
        c = lax.rem(k, 2)
        sib = k + 1 - 2 * c
        zbase = (g // nz) * nz
        zi = lax.rem(g, nz)

        def zpeer(d):
            return zbase + lax.rem(zi + d + nz, nz)

        def ypeer(d):
            return lax.rem(k + 2 * d + 8, 8)

        def term_peer(d):
            return lax.rem(k + d, 8)

        def x_peer(d):
            return lax.rem(g + nz * d, nsec)

        nxt = lax.rem(g + 1, nsec)
        prv = lax.rem(g + nsec - 1, nsec)

        def dev(kk, gg):
            return {"term": kk, "sector": gg}

        def remote(src, dst, s_sem, r_sem, kk, gg):
            return pltpu.make_async_remote_copy(
                src_ref=src, dst_ref=dst, send_sem=s_sem, recv_sem=r_sem,
                device_id=dev(kk, gg), device_id_type=MESH)

        barrier = pltpu.get_barrier_semaphore()
        beside = [(sib, g), (ypeer(1), g), (ypeer(-1), g), (k, x_peer(1)), (k, x_peer(nx - 1)),
                  (k, zpeer(1)), (k, zpeer(-1))]
        near = beside + [(k, nxt), (k, prv)]
        for p in near:
            pl.semaphore_signal(barrier, inc=1, device_id=dev(*p), device_id_type=MESH)

        dims_cp = pltpu.make_async_copy(dims_hbm, dims, int_sem.at[0])
        offs_cp = pltpu.make_async_copy(offsets_hbm, offsets, int_sem.at[1])
        dims_cp.start()
        offs_cp.start()
        vec_cp = [pltpu.make_async_copy(vectors.at[v], ext[v].at[pl.ds(2, 4)], vec_sem.at[v])
                  for v in range(NV)]
        for v in (1, 0, 2):
            vec_cp[v].start()
        renv_cp = pltpu.make_async_copy(renv, rbuf, env_sem.at[0])
        lenv_cp = pltpu.make_async_copy(lenv, lbuf, env_sem.at[1])

        dims_cp.wait()
        offs_cp.wait()
        masks = []
        row_id = lax.broadcasted_iota(jnp.int32, (256, 256), 0)
        col_id = lax.broadcasted_iota(jnp.int32, (256, 256), 1)
        for s in range(4):
            inside = (row_id < dims[0, s]) & (col_id < dims[1, s])
            masks.append(jnp.where(inside, 1.0, 0.0).astype(BF16))
        def masked(v):
            vec_cp[v].wait()
            for s in range(4):
                ext[v][2 + s] = ext[v][2 + s] * masks[s]

        masked(1)
        pl.semaphore_wait(barrier, len(near))

        def quarter(v, sector, yy):
            return ext[v].at[sector, pl.ds(pl.multiple_of(64 * yy, 64), 64)]

        def ahead(n, src, dst):
            cps = [remote(src(4 + c), dst(c), zs_sem.at[n, 0], zr_sem.at[n, 0], k, nxt),
                   remote(src(2 + c), dst(6 + c), zs_sem.at[n, 1], zr_sem.at[n, 1], k, prv)]
            for cp in cps:
                cp.start()
            return cps

        opp = lax.rem(y + 2, 4)
        z_own = ahead(3, lambda e: quarter(1, e, y), lambda e: quarter(1, e, y))
        masked(0)
        z_cp = {0: ahead(0, lambda e: ext[0].at[e], lambda e: ext[0].at[e])}
        z_cp[1] = ahead(1, lambda e: quarter(1, e, opp), lambda e: quarter(1, e, opp))
        masked(2)
        z_cp[2] = ahead(2, lambda e: ext[2].at[e], lambda e: ext[2].at[e])

        renv_cp.start()
        lenv_cp.start()

        chain = [beside,
                 [(sib, g), (ypeer(2), g), (k, x_peer(2)), (k, zpeer(2)), (k, zpeer(-2))],
                 [(ypeer(2), g), (k, zpeer(4)), (k, zpeer(-4))]]

        def tell(step):
            for p in chain[step]:
                pl.semaphore_signal(relay.at[step], inc=1, device_id=dev(*p), device_id_type=MESH)

        def hear(step):
            pl.semaphore_wait(relay.at[step], len(chain[step]))

        tell(0)

        sib_cp, y_cp = [], []

        def sib_send(v):
            cp = remote(part[v].at[:, :, 1 - c], sibrx.at[v], ss_sem.at[v], sr_sem.at[v], sib, g)
            cp.start()
            sib_cp.append(cp)

        def chip_sum(v):
            sib_cp[v].wait()
            for yy in range(4):
                for s in range(4):
                    both = part[v][s, yy, c].astype(F32) + sibrx[v, s, yy].astype(F32)
                    ysrc[v, yy, s] = both.astype(BF16)
            for d in (2, 1, 3):
                dest = lax.rem(y + d, 4)
                cp = remote(ysrc.at[v, dest], yrx.at[v, d - 1], ys_sem.at[v, d - 1], yr_sem.at[v, d - 1],
                            ypeer(d), g)
                cp.start()
                y_cp.append(cp)

        hear(0)
        tell(1)
        for cp in z_own:
            cp.wait_recv()
        h_cp = []
        for side, sector in enumerate((c, 6 + c)):
            for way, d in enumerate((1, -1)):
                cp = remote(quarter(1, sector, y), quarter(1, sector, y), hs_sem.at[side, way],
                            hr_sem.at[side, way], ypeer(d), g)
                cp.start()
                h_cp.append(cp)

        accs = {}
        passing = {}

        def pass_on(v):
            for cp in z_cp[v] + (h_cp if v == 1 else []):
                cp.wait_recv()
            passing[v] = [remote(ext[v].at[c], ext[v].at[c], fs_sem.at[v, 0], fr_sem.at[v, 0], sib, g),
                          remote(ext[v].at[6 + c], ext[v].at[6 + c], fs_sem.at[v, 1], fr_sem.at[v, 1], sib, g)]
            for cp in passing[v]:
                cp.start()

        def complete(v):
            for cp in passing[v]:
                cp.wait()
            if v == 1:
                for cp in h_cp:
                    cp.wait_send()

            @pl.when(g == 0)
            def _():
                ext[v][0:2] = jnp.zeros((2, 256, 256), BF16)

            @pl.when(g == nsec - 1)
            def _():
                ext[v][6:8] = jnp.zeros((2, 256, 256), BF16)

        def products(v, sectors):
            for s in sectors:
                tot = None
                for t in range(4):
                    inner = dot_nt(ext[v][2 + s - offsets[t]], rbuf[t, s]).astype(BF16)
                    term = jnp.dot(lbuf[t, s], inner, preferred_element_type=F32)
                    tot = term if tot is None else tot + term
                part[v][s] = tot.reshape(4, 2, 32, 256).astype(BF16)
                for i in range(NV):
                    z = ext[i][2 + s].astype(F32) * tot
                    z = jnp.sum(z.reshape(32, 8, 256), axis=0)
                    z = z[:, :128] + z[:, 128:]
                    accs[i, v] = z if s == 0 else accs[i, v] + z

        pass_on(0)
        hear(1)
        tell(2)
        renv_cp.wait()
        lenv_cp.wait()
        complete(0)
        products(0, (0, 1))
        pass_on(1)
        products(0, (2, 3))
        sib_send(0)
        complete(1)
        products(1, (0, 1))
        pass_on(2)
        products(1, (2, 3))
        sib_send(1)
        chip_sum(0)
        complete(2)
        products(2, (0, 1, 2, 3))
        sib_send(2)

        rows = jnp.concatenate(
            [jnp.sum(accs[i, j], axis=0, keepdims=True) for i in range(NV) for j in range(NV)], axis=0)
        sums = jnp.sum(rows, axis=1, keepdims=True)
        diag = (lax.broadcasted_iota(jnp.int32, (9, 128), 0)
                == lax.broadcasted_iota(jnp.int32, (9, 128), 1))
        ar1[0] = jnp.sum(jnp.where(diag, sums, 0.0), axis=0, keepdims=True)

        def spread(buf, sem, peers):
            for d, peer in peers:
                remote(buf.at[0], buf.at[d], as_sem.at[sem], a_sem.at[sem], *peer).start()

        def others(buf, sem):
            n = buf.shape[0] - 1
            return pltpu.make_async_copy(buf.at[pl.ds(1, n)], buf.at[pl.ds(1, n)], sem)

        hear(2)
        plane = sorted(((dx, dk) for dx in range(nx) for dk in range(8) if dx + dk),
                       key=lambda p: -(min(p[0], nx - p[0]) + min(p[1] // 2, 4 - p[1] // 2)))
        spread(ar1, 0, [(8 * dx + dk, (term_peer(dk), x_peer(dx))) for dx, dk in plane])
        chip_sum(1)
        chip_sum(2)
        others(ar1, a_sem.at[0]).wait()
        ar3[0] = jnp.sum(ar1[...], axis=0)
        line = sorted(range(1, nz), key=lambda d: -min(d, nz - d))
        spread(ar3, 1, [(d, (k, zpeer(d))) for d in line])

        lane = lax.broadcasted_iota(jnp.int32, (32, 256), 1)
        rown = lax.broadcasted_iota(jnp.int32, (32, 256), 0) + k * 32
        for v in range(NV):
            for j in range(3):
                y_cp[3 * v + j].wait()
            for s in range(4):
                tot = ysrc[v, y, s].astype(F32)
                for d in range(3):
                    tot = tot + yrx[v, d, s].astype(F32)
                inside = (rown < dims[0, s]) & (lane < dims[1, s])
                prod[v, s] = jnp.where(inside, tot, 0.0).astype(BF16)
        for cp in z_own + z_cp[0] + z_cp[1] + z_cp[2]:
            cp.wait_send()
        others(ar1, as_sem.at[0]).wait()
        others(ar3, as_sem.at[1]).wait()
        others(ar3, a_sem.at[1]).wait()
        sums = jnp.broadcast_to(jnp.sum(ar3[...], axis=0), (3, 128))
        r3 = lax.broadcasted_iota(jnp.int32, (3, 128), 0)
        l3 = lax.broadcasted_iota(jnp.int32, (3, 128), 1)
        full = jnp.zeros((3, 128), F32)
        for j in range(NV):
            col = jnp.sum(jnp.where(l3 == 3 * r3 + j, sums, 0.0), axis=1, keepdims=True)
            full = jnp.where(l3 == j, col, full)
        sub[...] = full[:, :3]

    return kernel


def hand_over(prod_in, sub_in, prod, sub, sem):
    cps = [pltpu.make_async_copy(prod_in, prod, sem.at[0]), pltpu.make_async_copy(sub_in, sub, sem.at[1])]
    for cp in cps:
        cp.start()
    for cp in cps:
        cp.wait()


def solution(mesh):
    nz = 16
    nx = mesh.shape["sector"] // nz
    vmem = pl.BlockSpec(memory_space=pltpu.VMEM)
    hbm = pl.BlockSpec(memory_space=pl.ANY)
    dma = pltpu.SemaphoreType.DMA

    def body(vectors, dims, offsets, left_env, right_env):
        prod, sub = pl.pallas_call(
            make_kernel(nz, nx),
            out_shape=(pltpu.VMEM((NV, 4, 32, 256), BF16), pltpu.VMEM((3, 3), F32)),
            in_specs=[hbm] * 5,
            out_specs=(vmem, vmem),
            scratch_shapes=(
                [pltpu.VMEM((8, 256, 256), BF16)] * 3
                + [pltpu.VMEM((4, 4, 2, 32, 256), BF16)] * 3
                + [pltpu.VMEM((4, 4, 256, 256), BF16)] * 2
                + [pltpu.VMEM((NV, 4, 4, 32, 256), BF16),
                   pltpu.VMEM((NV, 4, 4, 32, 256), BF16),
                   pltpu.VMEM((NV, 3, 4, 32, 256), BF16),
                   pltpu.VMEM((8 * nx, 1, 128), F32),
                   pltpu.VMEM((nz, 1, 128), F32),
                   pltpu.SMEM((2, 4), jnp.int32), pltpu.SMEM((4,), jnp.int32),
                   dma((NV,)), dma((2,)), dma((2,)),
                   dma((4, 2)), dma((4, 2)), dma((2, 2)), dma((2, 2)), dma((NV, 2)), dma((NV, 2)),
                   dma((NV,)), dma((NV,)), dma((NV, 3)), dma((NV, 3)),
                   dma((2,)), dma((2,)), pltpu.SemaphoreType.REGULAR((3,))]),
            compiler_params=pltpu.CompilerParams(
                collective_id=0, has_side_effects=True, vmem_limit_bytes=56 << 20),
        )(dims.T, offsets, vectors, left_env, right_env)
        return pl.pallas_call(
            hand_over,
            out_shape=(jax.ShapeDtypeStruct((NV, 4, 32, 256), BF16), jax.ShapeDtypeStruct((3, 3), F32)),
            in_specs=[vmem, vmem],
            out_specs=(hbm, hbm),
            scratch_shapes=[dma((2,))],
            compiler_params=pltpu.CompilerParams(vmem_limit_bytes=2 << 20),
        )(prod, sub)

    return jax.shard_map(
        body,
        mesh=mesh,
        in_specs=(
            P(None, "sector", None, None),
            P("sector", None),
            P("term"),
            P("term", "sector", None, None),
            P("term", "sector", None, None),
        ),
        out_specs=(P(None, "sector", "term", None), P()),
        check_vma=False,
    )
```
